32 devices in a mesh: tm: 8 (over z, x), head: 4 (over y, core).
Axes of the slice: x: 2, y: 2, z: 4, core: 2. Of those that a mesh axis runs over, the one named last changes fastest.
Arguments:
- query: bfloat16 [4096, 2560], P(('tm', 'head')), may hold values from -5 to 5, as said below
- keys: bfloat16 [4096, 2560], P(('tm', 'head')), may hold values from -5 to 5, as said below
- values: bfloat16 [4096, 2560], P(('tm', 'head')), may hold values from -6 to 6
- grad_out: bfloat16 [4096, 2560], P(('tm', 'head')), may hold values from -6 to 6
- tile_pattern: int32 [3, 4, 3], replicated, may hold values from 0 to 3, as said below
- window: int32 [8], replicated, may hold values from 1 to 3
Outputs:
- attended: bfloat16 [4096, 2560], P(('tm', 'head'))
- grad_query: bfloat16 [4096, 2560], P(('tm', 'head'))
- grad_keys: bfloat16 [4096, 2560], P(('tm', 'head'))
- grad_values: bfloat16 [4096, 2560], P(('tm', 'head'))
The draws below stay inside these ranges and needn't reach their ends.
Inputs may be any that keep to these rules, and one draw needn't show every extreme that they name: `query`: queries of the attention. `keys`: keys of the attention. `tile_pattern`: entry [l, q, 0] is q; the 3 entries of each row are distinct.
All inputs are finite; a program needn't handle non-finite values.
Results may differ from the reference program's by a relative error of at most 0.0091.
Values may be sent and summed in bfloat16 or wider, within the bound.
No kernel may reach another device: no remote copies, remote signals or barrier semaphores. Data moves between devices by JAX's collectives and lax.ppermute only.
A program may use at most 128 MiB of HBM per device.

```python
import math
import jax
import jax.numpy as jnp
from jax import lax

HD = 128
TILE = 128
QT = 4
SEL = 3
W = 3
FRAMES = 8
HEADS = 20
TOKENS = 4096
DA = 2560


def drawn_pair(key):
    base = jax.random.fold_in(key, 7)
    first, second = jax.random.split(base, 2)
    shape = (TOKENS, HEADS * HD)
    query = jnp.clip(jax.random.normal(first, shape, jnp.float32), -5.0, 5.0)
    keyset = jnp.clip(jax.random.normal(second, shape, jnp.float32), -5.0, 5.0)
    return (query, keyset)


def draw_query(key, part):
    return drawn_pair(key)[0].astype(jnp.bfloat16)


def draw_keys(key, part):
    return drawn_pair(key)[1].astype(jnp.bfloat16)


def draw_tile_pattern(key, part):
    base = jax.random.fold_in(key, 13)
    row_keys = jax.random.split(base, W * QT)
    others = jax.vmap(lambda row_key: jax.random.permutation(row_key, QT - 1)[:SEL - 1])(row_keys)
    others = others.reshape(W, QT, SEL - 1)
    own = jnp.broadcast_to(jnp.arange(QT, dtype=jnp.int32)[None, :, None], (W, QT, 1))
    picked = (own + 1 + others) % QT
    return jnp.concatenate([own, picked], -1).astype(jnp.int32)


def draw_window(key, part):
    base = jax.random.fold_in(key, 11)
    first, second = jax.random.split(base, 2)
    widths = jax.random.randint(first, (FRAMES,), 1, W + 1)
    spots = jax.random.permutation(second, FRAMES)
    widths = widths.at[spots[0]].set(W).at[spots[1]].set(1)
    return widths.astype(jnp.int32)


def levels(own_key, extent, cuts, low, largest):
    level = 1.0
    for dim, blocks in cuts:
        steps = jax.random.uniform(jax.random.fold_in(jax.random.fold_in(own_key, 6), dim), (blocks,), jnp.float32, low / len(cuts), largest / len(cuts))
        level = level * jnp.repeat(jnp.exp(steps), extent[dim] // blocks).reshape((-1,) + (1,) * (len(extent) - 1 - dim))
    return level


def scatter_about(rng, dims, scale, most, cuts=(), kind=jnp.bfloat16):
    level = levels(rng, dims, cuts, -0.22, 0.18) if cuts else 1.0
    values = jax.random.normal(rng, dims, jnp.float32) * scale * level
    return jnp.minimum(jnp.maximum(values, -most), most).astype(kind)


def setup_inputs(seed: int = 0) -> dict:
    arg_keys = jax.random.split(jax.random.key(seed), 7)
    query = draw_query(jax.random.fold_in(arg_keys[6], 71), 0)
    keys = draw_keys(jax.random.fold_in(arg_keys[6], 71), 0)
    values = scatter_about(arg_keys[2], (TOKENS, DA), 1.0, 6.0, ((0, 32),))
    grad_out = scatter_about(arg_keys[3], (TOKENS, DA), 1.0, 6.0, ((0, 32),))
    tile_pattern = draw_tile_pattern(jax.random.fold_in(arg_keys[6], 71), 0)
    window = draw_window(jax.random.fold_in(arg_keys[6], 71), 0)
    return {"query": query, "keys": keys, "values": values, "grad_out": grad_out, "tile_pattern": tile_pattern, "window": window}


NEG = -1e+30

def frame_pass(q_head, k_head, v_head, g_head, tile_pattern, window, frame):
    scale = 1.0 / math.sqrt(HD)
    highest = lax.Precision.HIGHEST
    query = lax.dynamic_index_in_dim(q_head, frame, 0, False).astype(jnp.float32)
    grad = lax.dynamic_index_in_dim(g_head, frame, 0, False).astype(jnp.float32)
    key_parts = []
    val_parts = []
    for lag in range(W):
        source = jnp.maximum(frame - lag, 0).astype(jnp.int32)
        key_frame = lax.dynamic_index_in_dim(k_head, source, 0, False)
        val_frame = lax.dynamic_index_in_dim(v_head, source, 0, False)
        key_parts.append(jnp.take(key_frame, tile_pattern[lag], axis=0))
        val_parts.append(jnp.take(val_frame, tile_pattern[lag], axis=0))
    count = W * SEL * TILE
    keyset = jnp.stack(key_parts, 1).reshape(QT, count, HD).astype(jnp.float32)
    valset = jnp.stack(val_parts, 1).reshape(QT, count, HD).astype(jnp.float32)
    lags = jnp.arange(W, dtype=jnp.int32)
    limit = window[frame]
    live = (lags <= frame) & (lags < limit)
    live_cols = jnp.repeat(live, SEL * TILE)
    scores = jnp.einsum('qad,qbd->qab', query, keyset) * scale
    scores = jnp.where(live_cols, scores, NEG)
    top = lax.optimization_barrier(jnp.max(scores, -1, keepdims=True))
    expo = jnp.exp(scores - top)
    prob = expo / lax.optimization_barrier(jnp.sum(expo, -1, keepdims=True))
    prob_b = lax.optimization_barrier(prob.astype(jnp.bfloat16)).astype(jnp.float32)
    output = jnp.einsum('qab,qbd->qad', prob_b, valset)
    delta = lax.optimization_barrier(jnp.sum(grad * output, -1, keepdims=True))
    dprob = jnp.einsum('qad,qbd->qab', grad, valset)
    dscore = lax.optimization_barrier((prob * (dprob - delta) * scale).astype(jnp.bfloat16)).astype(jnp.float32)
    dquery = jnp.einsum('qab,qbd->qad', dscore, keyset)
    dkeys = jnp.einsum('qab,qad->qbd', dscore, query).reshape(QT, W, SEL, TILE, HD)
    dvals = jnp.einsum('qab,qad->qbd', prob_b, grad).reshape(QT, W, SEL, TILE, HD)
    onehot = (tile_pattern[:, :, :, None] == jnp.arange(QT, dtype=jnp.int32)).astype(jnp.float32)
    spread_k = jnp.einsum('qwstd,wqsk->wktd', dkeys, onehot, precision=highest)
    spread_v = jnp.einsum('qwstd,wqsk->wktd', dvals, onehot, precision=highest)
    return (output.astype(jnp.bfloat16), dquery.astype(jnp.bfloat16), spread_k[0], spread_v[0], spread_k[1:], spread_v[1:])

def shift_up(array):
    padding = jnp.zeros((1,) + array.shape[1:], jnp.float32)
    return jnp.concatenate([array[1:], padding], 0)

def round_trip(array):
    return lax.optimization_barrier(array.astype(jnp.bfloat16)).astype(jnp.float32)

def head_pass(q_head, k_head, v_head, g_head, tile_pattern, window):
    frames = jnp.arange(FRAMES, dtype=jnp.int32)
    results = lax.map(lambda frame: frame_pass(q_head, k_head, v_head, g_head, tile_pattern, window, frame), frames)
    output, dquery, own_k, own_v, far_k, far_v = results
    pending_k = round_trip(far_k[:, W - 2])
    pending_v = round_trip(far_v[:, W - 2])
    for lag in range(W - 1, 0, -1):
        moved_k = shift_up(pending_k)
        moved_v = shift_up(pending_v)
        if lag > 1:
            pending_k = round_trip(far_k[:, lag - 2] + moved_k)
            pending_v = round_trip(far_v[:, lag - 2] + moved_v)
        else:
            pending_k = moved_k
            pending_v = moved_v
    total_k = own_k + pending_k
    total_v = own_v + pending_v
    return (output, dquery, total_k.astype(jnp.bfloat16), total_v.astype(jnp.bfloat16))

def split_heads(array):
    return jnp.transpose(array.reshape(FRAMES, QT, TILE, HEADS, HD), (3, 0, 1, 2, 4))

def join_heads(array):
    return jnp.transpose(array, (1, 2, 3, 0, 4)).reshape(TOKENS, HEADS * HD)

def reference(query, keys, values, grad_out, tile_pattern, window):
    groups = (split_heads(query), split_heads(keys), split_heads(values), split_heads(grad_out))
    results = lax.map(lambda group: head_pass(group[0], group[1], group[2], group[3], tile_pattern, window), groups)
    return (join_heads(results[0]), join_heads(results[1]), join_heads(results[2]), join_heads(results[3]))
```

```python
import math

import jax
import jax.numpy as jnp
from jax import lax
from jax.experimental import pallas as pl
from jax.experimental.pallas import tpu as pltpu
from jax.sharding import PartitionSpec as P

HD = 128
QT = 4
SEL = 3
W = 3
GROUP = 2
CORES = 2
SLOTS = 4
CHUNKS = (2, 3)
NEG = -1e30
AXES = ("tm", "head")


def params(limit=32):
    return pltpu.CompilerParams(vmem_limit_bytes=limit * 2**20)


def moved(block, to):
    frames, heads = lax.axis_size("tm"), lax.axis_size("head")
    route = []
    for t in range(frames):
        for h in range(heads):
            t2, h2 = to(t, h)
            if 0 <= t2 < frames:
                route.append((t * heads + h, t2 * heads + h2))
    return lax.ppermute(block, AXES, route)


def to_slot(block, slot):
    return moved(block, lambda t, h: (t ^ (slot // 2), h ^ (slot % 2 * CORES)))


def to_core(block):
    return moved(block, lambda t, h: (t, h ^ 1))


def to_group(block, step):
    return moved(block, lambda t, h: (t + step * GROUP, h))


def place():
    t, h = lax.axis_index("tm"), lax.axis_index("head")
    return t // GROUP, t % GROUP, h // CORES, h % CORES


def where_am_i():
    t, h = lax.axis_index("tm"), lax.axis_index("head")
    return jnp.stack([t, h]).astype(jnp.int32)


def pack_kernel(chunks, per_chip, me, a_ref, b_ref, *outs):
    x, y = me[0] % GROUP, me[1] // CORES
    tiles = a_ref.shape[1] // (HD * per_chip * GROUP)
    n = 0
    start = 0
    for nh in chunks:
        for slot in range(SLOTS):
            chip = (x ^ (slot // 2)) * tiles + (y ^ (slot % 2))
            for h in range(nh):
                col = pl.multiple_of((chip * per_chip + start + h) * HD, HD)
                outs[n][0, h] = a_ref[:, pl.ds(col, HD)]
                outs[n][1, h] = b_ref[:, pl.ds(col, HD)]
            n += 1
        start += nh


def pack(me, a, b, chunks, per_chip):
    rows = a.shape[0]
    shapes = [
        jax.ShapeDtypeStruct((2, nh, rows, HD), a.dtype) for nh in chunks for _ in range(SLOTS)
    ]
    vmem = pl.BlockSpec(memory_space=pltpu.VMEM)
    outs = pl.pallas_call(
        lambda *refs: pack_kernel(chunks, per_chip, *refs),
        out_shape=shapes,
        in_specs=[pl.BlockSpec(memory_space=pltpu.SMEM), vmem, vmem],
        out_specs=[vmem] * len(shapes),
        compiler_params=params(),
    )(me, a, b)
    return [outs[i * SLOTS : (i + 1) * SLOTS] for i in range(len(chunks))]


def unpack_kernel(chunks, per_chip, me, *refs):
    a_ref, b_ref = refs[-2:]
    x, y = me[0] % GROUP, me[1] // CORES
    tiles = a_ref.shape[1] // (HD * per_chip * GROUP)
    n = 0
    start = 0
    for nh in chunks:
        for slot in range(SLOTS):
            chip = (x ^ (slot // 2)) * tiles + (y ^ (slot % 2))
            for h in range(nh):
                col = pl.multiple_of((chip * per_chip + start + h) * HD, HD)
                a_ref[:, pl.ds(col, HD)] = refs[n][0, h]
                b_ref[:, pl.ds(col, HD)] = refs[n][1, h]
            n += 1
        start += nh


def unpack(me, pieces, chunks, per_chip, width):
    flat = [p for group in pieces for p in group]
    rows = flat[0].shape[2]
    vmem = pl.BlockSpec(memory_space=pltpu.VMEM)
    return pl.pallas_call(
        lambda *refs: unpack_kernel(chunks, per_chip, *refs),
        out_shape=[jax.ShapeDtypeStruct((rows, width), flat[0].dtype)] * 2,
        in_specs=[pl.BlockSpec(memory_space=pltpu.SMEM)] + [vmem] * len(flat),
        out_specs=[vmem] * 2,
        compiler_params=params(),
    )(me, *flat)


def dot(a, b, dims):
    return lax.dot_general(a, b, (dims, ((), ())), preferred_element_type=jnp.float32)


def attend_kernel(me, tp, win, *refs):
    kv_refs = refs[:4]
    qg_refs = refs[4:8]
    aq_refs = refs[8:12]
    own_f, halo_f, own_b, halo_b = refs[12:16]
    kv, ksel, vsel, acc = refs[16:]
    group, x = me[0] // GROUP, me[0] % GROUP
    y, core = me[1] // CORES, me[1] % CORES
    scale = 1.0 / math.sqrt(HD)
    c2 = scale * math.log2(math.e)
    for part in range(4):
        for s in range(SLOTS):
            kv[part * SLOTS + s] = kv_refs[part][s]
    acc[...] = jnp.zeros_like(acc)
    for j in range(SLOTS):
        q = qg_refs[j][0]
        g = qg_refs[j][1]
        xq = x ^ (j // 2)
        tile = (y ^ (j % 2)) * CORES + core
        frame = group * GROUP + xq
        limit = win[frame]
        slots = []
        biases = []
        for lag in range(W):
            rest = xq - lag
            plane = jnp.where(rest < 0, 1, 0)
            dx = (rest & 1) ^ x
            live = (lag <= frame) & (lag < limit)
            biases.append(jnp.where(live, 0.0, NEG))
            for i in range(SEL):
                t = tp[lag, tile, i]
                dc = (t % CORES) ^ core
                dy = (t // CORES) ^ y
                slot = plane * 8 + dc * 4 + dx * 2 + dy
                at = (lag * SEL + i) * HD
                ksel[j, at : at + HD] = kv[slot, 0]
                vsel[j, at : at + HD] = kv[slot, 1]
                slots.append(slot)
        span = SEL * HD
        k_all, v_all = ksel[j], vsel[j]
        s = dot(q, k_all, ((1,), (1,))) * c2
        s = jnp.concatenate(
            [s[:, lag * span : (lag + 1) * span] + biases[lag] for lag in range(W)], 1
        )
        top = jnp.max(s, -1, keepdims=True)
        e = jnp.exp2(s - top)
        prob = e * (1.0 / jnp.sum(e, -1, keepdims=True))
        prob_b = prob.astype(jnp.bfloat16)
        out = dot(prob_b, v_all, ((1,), (0,)))
        delta = jnp.sum(g.astype(jnp.float32) * out, -1, keepdims=True)
        dprob = dot(g, v_all, ((1,), (1,)))
        ds = (prob * (dprob - delta)).astype(jnp.bfloat16)
        aq_refs[j][0] = out.astype(jnp.bfloat16)
        aq_refs[j][1] = (dot(ds, k_all, ((1,), (0,))) * scale).astype(jnp.bfloat16)
        dk = dot(q, ds, ((0,), (0,)))
        dv = dot(g, prob_b, ((0,), (0,)))
        for i, slot in enumerate(slots):
            acc[slot, 0] += dk[:, i * HD : (i + 1) * HD]
            acc[slot, 1] += dv[:, i * HD : (i + 1) * HD]
    for part, ref in enumerate((own_f, own_b, halo_f, halo_b)):
        for s in range(SLOTS):
            ref[s, 0] = (acc[part * SLOTS + s, 0].T * scale).astype(ref.dtype)
            ref[s, 1] = acc[part * SLOTS + s, 1].T.astype(ref.dtype)


def attend(me, tp, win, own, other, halo, halo_other, qg):
    nh, rows = own.shape[2], own.shape[3]
    smem = pl.BlockSpec(memory_space=pltpu.SMEM)
    kv_spec = pl.BlockSpec((SLOTS, 2, None, rows, HD), lambda h: (0, 0, h, 0, 0))
    qg_spec = pl.BlockSpec((2, None, rows, HD), lambda h: (0, h, 0, 0))
    kv_shape = (SLOTS, 2, nh, rows, HD)
    bf, f32 = jnp.bfloat16, jnp.float32
    count = W * SEL * rows
    outs = pl.pallas_call(
        attend_kernel,
        grid=(nh,),
        out_shape=[jax.ShapeDtypeStruct((2, nh, rows, HD), bf)] * 4
        + [jax.ShapeDtypeStruct(kv_shape, t) for t in (f32, f32, bf, bf)],
        in_specs=[smem] * 3 + [kv_spec] * 4 + [qg_spec] * 4,
        out_specs=[qg_spec] * 4 + [kv_spec] * 4,
        scratch_shapes=[
            pltpu.VMEM((4 * SLOTS, 2, rows, HD), bf),
            pltpu.VMEM((SLOTS, count, HD), bf),
            pltpu.VMEM((SLOTS, count, HD), bf),
            pltpu.VMEM((4 * SLOTS, 2, HD, rows), f32),
        ],
        compiler_params=params(),
        cost_estimate=pl.CostEstimate(
            flops=nh * SLOTS * 12 * rows * count * HD,
            bytes_accessed=nh * rows * HD * 2 * 72,
            transcendentals=nh * SLOTS * rows * count,
        ),
    )(me, tp, win, own, other, halo, halo_other, *qg)
    return outs[:4], outs[4:]


def shards(query, keys, values, grad_out, tile_pattern, window):
    width = query.shape[1]
    per_chip = width // HD // (GROUP * (lax.axis_size("head") // CORES))
    chunks = CHUNKS if sum(CHUNKS) == per_chip else (per_chip,)
    me = where_am_i()
    f32, bf = jnp.float32, jnp.bfloat16
    kv_sent = pack(me, keys, values, chunks, per_chip)
    qg_sent = pack(me, query, grad_out, chunks, per_chip)
    out_pieces, grad_pieces = [], []
    for i in range(len(chunks)):
        kv = [kv_sent[i][0]] + [to_slot(kv_sent[i][s], s) for s in range(1, SLOTS)]
        qg = [qg_sent[i][0]] + [to_slot(qg_sent[i][s], s) for s in range(1, SLOTS)]
        own = jnp.stack(kv)
        halo = to_group(own, 1)
        other = to_core(own)
        halo_other = to_core(halo)
        aq, (own_f, halo_f, own_b, halo_b) = attend(
            me, tile_pattern, window, own, other, halo, halo_other, qg
        )
        back = (halo_f + to_core(halo_b).astype(f32)).astype(bf)
        later = to_group(back, -1)
        mine = to_core(own_b)
        out_pieces.append([aq[0]] + [to_slot(aq[s], s) for s in range(1, SLOTS)])
        total = [
            (own_f[s] + mine[s].astype(f32) + later[s].astype(f32)).astype(bf)
            for s in range(SLOTS)
        ]
        grad_pieces.append([total[0]] + [to_slot(total[s], s) for s in range(1, SLOTS)])
    attended, grad_query = unpack(me, out_pieces, chunks, per_chip, width)
    grad_keys, grad_values = unpack(me, grad_pieces, chunks, per_chip, width)
    return (attended, grad_query, grad_keys, grad_values)


def solution(mesh):
    placed = P(AXES, None)
    return jax.shard_map(
        shards,
        mesh=mesh,
        in_specs=(placed,) * 4 + (P(), P()),
        out_specs=(placed,) * 4,
        check_vma=False,
    )
```

```python
import math

import jax
import jax.numpy as jnp
from jax import lax
from jax.experimental import pallas as pl
from jax.experimental.pallas import tpu as pltpu
from jax.sharding import PartitionSpec as P

HD = 128
QT = 4
SEL = 3
W = 3
GROUP = 2
CORES = 2
SLOTS = 4
FIRST = 2
NEG = -1e30
AXES = ("tm", "head")


def params(limit=32):
    return pltpu.CompilerParams(vmem_limit_bytes=limit * 2**20)


def moved(block, to):
    frames, heads = lax.axis_size("tm"), lax.axis_size("head")
    route = []
    for t in range(frames):
        for h in range(heads):
            t2, h2 = to(t, h)
            if 0 <= t2 < frames:
                route.append((t * heads + h, t2 * heads + h2))
    return lax.ppermute(block, AXES, route)


def to_slot(block, slot):
    return moved(block, lambda t, h: (t ^ (slot // 2), h ^ (slot % 2 * CORES)))


def to_core(block):
    return moved(block, lambda t, h: (t, h ^ 1))


def to_group(block, step):
    return moved(block, lambda t, h: (t + step * GROUP, h))


def place():
    t, h = lax.axis_index("tm"), lax.axis_index("head")
    return t // GROUP, t % GROUP, h // CORES, h % CORES


def where_am_i():
    t, h = lax.axis_index("tm"), lax.axis_index("head")
    return jnp.stack([t, h]).astype(jnp.int32)


def columns(me, ref, per_chip, slot):
    x, y = me[0] % GROUP, me[1] // CORES
    tiles = ref.shape[1] // (HD * per_chip * GROUP)
    chip = (x ^ (slot // 2)) * tiles + (y ^ (slot % 2))
    return lambda head: pl.ds(pl.multiple_of((chip * per_chip + head) * HD, HD), HD)


def pack_kernel(plan, per_chip, used, me, *refs):
    outs = refs[used:]
    for slot in range(SLOTS):
        at = columns(me, refs[0], per_chip, slot)
        for n, (first, head) in enumerate(plan):
            outs[slot][n, 0] = refs[first][:, at(head)]
            outs[slot][n, 1] = refs[first + 1][:, at(head)]


def pack(me, arrays, plan, per_chip, after=()):
    rows = arrays[0].shape[0]
    shape = jax.ShapeDtypeStruct((len(plan), 2, rows, HD), arrays[0].dtype)
    vmem = pl.BlockSpec(memory_space=pltpu.VMEM)
    used = len(arrays) + len(after)
    return pl.pallas_call(
        lambda *refs: pack_kernel(plan, per_chip, used, *refs),
        out_shape=[shape] * SLOTS,
        in_specs=[pl.BlockSpec(memory_space=pltpu.SMEM)]
        + [vmem] * len(arrays)
        + [pl.BlockSpec(memory_space=pl.ANY)] * len(after),
        out_specs=[vmem] * SLOTS,
        compiler_params=params(),
    )(me, *arrays, *after)


def unpack_kernel(places, per_chip, me, *refs):
    a_ref, b_ref = refs[-2:]
    for slot in range(SLOTS):
        at = columns(me, a_ref, per_chip, slot)
        for head, (group, n) in enumerate(places):
            ref = refs[group * SLOTS + slot]
            a_ref[:, at(head)] = ref[n, 0]
            b_ref[:, at(head)] = ref[n, 1]


def unpack(me, groups, places, per_chip, width):
    flat = [p for group in groups for p in group]
    rows = flat[0].shape[2]
    vmem = pl.BlockSpec(memory_space=pltpu.VMEM)
    return pl.pallas_call(
        lambda *refs: unpack_kernel(places, per_chip, *refs),
        out_shape=[jax.ShapeDtypeStruct((rows, width), flat[0].dtype)] * 2,
        in_specs=[pl.BlockSpec(memory_space=pltpu.SMEM)] + [vmem] * len(flat),
        out_specs=[vmem] * 2,
        compiler_params=params(),
    )(me, *flat)


def dot(a, b, dims):
    return lax.dot_general(a, b, (dims, ((), ())), preferred_element_type=jnp.float32)


def attend_kernel(me, tp, win, *refs):
    kv_refs = refs[:4]
    qg_refs = refs[4:8]
    aq_refs = refs[8:12]
    own_f, halo_f, sent_b = refs[12:15]
    kv, ksel, vsel, acc = refs[15:]
    group, x = me[0] // GROUP, me[0] % GROUP
    y, core = me[1] // CORES, me[1] % CORES
    scale = 1.0 / math.sqrt(HD)
    c2 = scale * math.log2(math.e)
    for part in range(4):
        for s in range(SLOTS):
            kv[part * SLOTS + s] = kv_refs[part][s]
    acc[...] = jnp.zeros_like(acc)
    for j in range(SLOTS):
        q = qg_refs[j][0]
        g = qg_refs[j][1]
        xq = x ^ (j // 2)
        tile = (y ^ (j % 2)) * CORES + core
        frame = group * GROUP + xq
        limit = win[frame]
        slots = []
        biases = []
        for lag in range(W):
            rest = xq - lag
            plane = jnp.where(rest < 0, 1, 0)
            dx = (rest & 1) ^ x
            live = (lag <= frame) & (lag < limit)
            biases.append(jnp.where(live, 0.0, NEG))
            for i in range(SEL):
                t = tp[lag, tile, i]
                dc = (t % CORES) ^ core
                dy = (t // CORES) ^ y
                slot = plane * 8 + dc * 4 + dx * 2 + dy
                at = (lag * SEL + i) * HD
                ksel[j, at : at + HD] = kv[slot, 0]
                vsel[j, at : at + HD] = kv[slot, 1]
                slots.append(slot)
        span = SEL * HD
        k_all, v_all = ksel[j], vsel[j]
        s = dot(q, k_all, ((1,), (1,))) * c2
        s = jnp.concatenate(
            [s[:, lag * span : (lag + 1) * span] + biases[lag] for lag in range(W)], 1
        )
        top = jnp.max(s, -1, keepdims=True)
        e = jnp.exp2(s - top)
        prob = e * (1.0 / jnp.sum(e, -1, keepdims=True))
        prob_b = prob.astype(jnp.bfloat16)
        out = dot(prob_b, v_all, ((1,), (0,)))
        delta = jnp.sum(g.astype(jnp.float32) * out, -1, keepdims=True)
        dprob = dot(g, v_all, ((1,), (1,)))
        ds = (prob * (dprob - delta)).astype(jnp.bfloat16)
        aq_refs[j][0] = out.astype(jnp.bfloat16)
        aq_refs[j][1] = (dot(ds, k_all, ((1,), (0,))) * scale).astype(jnp.bfloat16)
        dk = dot(q, ds, ((0,), (0,)))
        dv = dot(g, prob_b, ((0,), (0,)))
        for i, slot in enumerate(slots):
            acc[slot, 0] += dk[:, i * HD : (i + 1) * HD]
            acc[slot, 1] += dv[:, i * HD : (i + 1) * HD]
    for part, (ref, to) in enumerate(((own_f, 0), (sent_b, 0), (halo_f, 0), (sent_b, SLOTS))):
        for s in range(SLOTS):
            ref[to + s, 0] = (acc[part * SLOTS + s, 0].T * scale).astype(ref.dtype)
            ref[to + s, 1] = acc[part * SLOTS + s, 1].T.astype(ref.dtype)


def attend(me, tp, win, own, other, halo, halo_other, qg, qg_at):
    nh, rows = own.shape[1], own.shape[3]
    smem = pl.BlockSpec(memory_space=pltpu.SMEM)
    kv_spec = pl.BlockSpec((SLOTS, None, 2, rows, HD), lambda h: (0, h, 0, 0, 0))
    both_spec = pl.BlockSpec((2 * SLOTS, None, 2, rows, HD), lambda h: (0, h, 0, 0, 0))
    qg_spec = pl.BlockSpec((None, 2, rows, HD), lambda h: (h + qg_at, 0, 0, 0))
    aq_spec = pl.BlockSpec((None, 2, rows, HD), lambda h: (h, 0, 0, 0))
    bf, f32 = jnp.bfloat16, jnp.float32
    count = W * SEL * rows
    outs = pl.pallas_call(
        attend_kernel,
        grid=(nh,),
        out_shape=[jax.ShapeDtypeStruct((nh, 2, rows, HD), bf)] * 4
        + [
            jax.ShapeDtypeStruct((SLOTS, nh, 2, rows, HD), f32),
            jax.ShapeDtypeStruct((SLOTS, nh, 2, rows, HD), f32),
            jax.ShapeDtypeStruct((2 * SLOTS, nh, 2, rows, HD), bf),
        ],
        in_specs=[smem] * 3 + [kv_spec] * 4 + [qg_spec] * 4,
        out_specs=[aq_spec] * 4 + [kv_spec] * 2 + [both_spec],
        scratch_shapes=[
            pltpu.VMEM((4 * SLOTS, 2, rows, HD), bf),
            pltpu.VMEM((SLOTS, count, HD), bf),
            pltpu.VMEM((SLOTS, count, HD), bf),
            pltpu.VMEM((4 * SLOTS, 2, HD, rows), f32),
        ],
        compiler_params=params(),
        cost_estimate=pl.CostEstimate(flops=1, bytes_accessed=1, transcendentals=0),
    )(me, tp, win, own, other, halo, halo_other, *qg)
    return outs[:4], outs[4:]


def exchange(pieces):
    return [pieces[0]] + [to_slot(pieces[s], s) for s in range(1, SLOTS)]


def shards(query, keys, values, grad_out, tile_pattern, window):
    width = query.shape[1]
    per_chip = width // HD // (GROUP * (lax.axis_size("head") // CORES))
    na = min(FIRST, per_chip - 1)
    nb = per_chip - na
    me = where_am_i()
    f32, bf = jnp.float32, jnp.bfloat16
    heads = range(per_chip)

    def summed(own_f, mine, later):
        return [
            (own_f[s] + mine[s].astype(f32) + later[s].astype(f32)).astype(bf)
            for s in range(SLOTS)
        ]

    def backward(halo_f, sent_b):
        mine = to_core(sent_b)
        back = (halo_f + mine[SLOTS:].astype(f32)).astype(bf)
        return mine, back, to_group(back, -1)

    kv_a = exchange(pack(me, [keys, values], [(0, h) for h in heads[:na]], per_chip))
    own_a = jnp.stack(kv_a)
    halo_a = to_group(own_a, 1)
    other_a = to_core(own_a)
    mixed = exchange(
        pack(
            me,
            [query, grad_out, keys, values],
            [(0, h) for h in heads[:na]] + [(2, h) for h in heads[na:]],
            per_chip,
            after=kv_a[1:],
        )
    )
    mixed, halo_a = lax.optimization_barrier((mixed, halo_a))
    own_b = jnp.stack([p[na:] for p in mixed])
    halo_b = to_group(own_b, 1)
    other_b = to_core(own_b)
    qg_b = exchange(
        pack(me, [query, grad_out], [(0, h) for h in heads[na:]], per_chip, after=mixed[1:])
    )
    halo_other_a = to_core(halo_a)
    aq_a, (own_fa, halo_fa, sent_a) = attend(
        me, tile_pattern, window, own_a, other_a, halo_a, halo_other_a, mixed, 0
    )
    sent_a, qg_b, halo_b = lax.optimization_barrier((sent_a, qg_b, halo_b))
    mine_a, back_a, later_a = backward(halo_fa, sent_a)
    got_aq_a = exchange(aq_a)
    halo_other_b = to_core(halo_b)
    qg_b, back_a = lax.optimization_barrier((qg_b, back_a))
    aq_b, (own_fb, halo_fb, sent_b) = attend(
        me, tile_pattern, window, own_b, other_b, halo_b, halo_other_b, qg_b, 0
    )
    sent_b, later_a, got_aq_a = lax.optimization_barrier((sent_b, later_a, got_aq_a))
    mine_b, _, later_b = backward(halo_fb, sent_b)
    total_a = summed(own_fa, mine_a, later_a)
    got_mixed = exchange([jnp.concatenate([aq_b[s], total_a[s]]) for s in range(SLOTS)])
    attended, grad_query = unpack(
        me,
        [got_aq_a, got_mixed],
        [(0, n) for n in range(na)] + [(1, n) for n in range(nb)],
        per_chip,
        width,
    )
    got_b = exchange(summed(own_fb, mine_b, later_b))
    grad_keys, grad_values = unpack(
        me,
        [got_mixed, got_b],
        [(0, nb + n) for n in range(na)] + [(1, n) for n in range(nb)],
        per_chip,
        width,
    )
    return (attended, grad_query, grad_keys, grad_values)


def solution(mesh):
    placed = P(AXES, None)
    return jax.shard_map(
        shards,
        mesh=mesh,
        in_specs=(placed,) * 4 + (P(), P()),
        out_specs=(placed,) * 4,
        check_vma=False,
    )
```

```python
import math

import jax
import jax.numpy as jnp
from jax import lax
from jax.experimental import pallas as pl
from jax.experimental.pallas import tpu as pltpu
from jax.sharding import PartitionSpec as P

HD = 128
QT = 4
SEL = 3
W = 3
GROUP = 2
CORES = 2
SLOTS = 4
FIRST = 2
NEG = -1e30
AXES = ("tm", "head")


def params(limit=32):
    return pltpu.CompilerParams(vmem_limit_bytes=limit * 2**20)


def moved(block, to):
    frames, heads = lax.axis_size("tm"), lax.axis_size("head")
    route = []
    for t in range(frames):
        for h in range(heads):
            t2, h2 = to(t, h)
            route.append((t * heads + h, t2 % frames * heads + h2))
    return lax.ppermute(block, AXES, route)


def to_slot(block, slot):
    return moved(block, lambda t, h: (t ^ (slot // 2), h ^ (slot % 2 * CORES)))


def to_core(block):
    return moved(block, lambda t, h: (t, h ^ 1))


def to_group(block, step):
    return moved(block, lambda t, h: (t + step * GROUP, h))


def place():
    t, h = lax.axis_index("tm"), lax.axis_index("head")
    return t // GROUP, t % GROUP, h // CORES, h % CORES


def where_am_i():
    t, h = lax.axis_index("tm"), lax.axis_index("head")
    return jnp.stack([t, h]).astype(jnp.int32)


def columns(me, ref, per_chip, slot):
    x, y = me[0] % GROUP, me[1] // CORES
    tiles = ref.shape[1] // (HD * per_chip * GROUP)
    chip = (x ^ (slot // 2)) * tiles + (y ^ (slot % 2))
    return lambda head: pl.ds(pl.multiple_of((chip * per_chip + head) * HD, HD), HD)


def pack_kernel(plan, per_chip, used, me, *refs):
    outs = refs[used:]
    for slot in range(SLOTS):
        at = columns(me, refs[0], per_chip, slot)
        for n, (first, head) in enumerate(plan):
            outs[slot][n, 0] = refs[first][:, at(head)]
            outs[slot][n, 1] = refs[first + 1][:, at(head)]


def pack(me, arrays, plan, per_chip, after=()):
    rows = arrays[0].shape[0]
    shape = jax.ShapeDtypeStruct((len(plan), 2, rows, HD), arrays[0].dtype)
    vmem = pl.BlockSpec(memory_space=pltpu.VMEM)
    used = len(arrays) + len(after)
    return pl.pallas_call(
        lambda *refs: pack_kernel(plan, per_chip, used, *refs),
        out_shape=[shape] * SLOTS,
        in_specs=[pl.BlockSpec(memory_space=pltpu.SMEM)]
        + [vmem] * len(arrays)
        + [pl.BlockSpec(memory_space=pl.ANY)] * len(after),
        out_specs=[vmem] * SLOTS,
        compiler_params=params(),
    )(me, *arrays, *after)


def unpack_kernel(places, per_chip, me, *refs):
    a_ref, b_ref = refs[-2:]
    for slot in range(SLOTS):
        at = columns(me, a_ref, per_chip, slot)
        for head, (group, n) in enumerate(places):
            ref = refs[group * SLOTS + slot]
            a_ref[:, at(head)] = ref[n, 0]
            b_ref[:, at(head)] = ref[n, 1]


def unpack(me, groups, places, per_chip, width):
    flat = [p for group in groups for p in group]
    rows = flat[0].shape[2]
    vmem = pl.BlockSpec(memory_space=pltpu.VMEM)
    return pl.pallas_call(
        lambda *refs: unpack_kernel(places, per_chip, *refs),
        out_shape=[jax.ShapeDtypeStruct((rows, width), flat[0].dtype)] * 2,
        in_specs=[pl.BlockSpec(memory_space=pltpu.SMEM)] + [vmem] * len(flat),
        out_specs=[vmem] * 2,
        compiler_params=params(),
    )(me, *flat)


def dot(a, b, dims):
    return lax.dot_general(a, b, (dims, ((), ())), preferred_element_type=jnp.float32)


def attend_kernel(me, tp, win, *refs):
    kv_refs = refs[:4]
    qg_refs = refs[4:8]
    aq_refs = refs[8:12]
    own_f, halo_f, sent_b = refs[12:15]
    kv, qg, aq, scaled, ksel, vsel, probs, dscores = refs[15:]
    group, x = me[0] // GROUP, me[0] % GROUP
    y, core = me[1] // CORES, me[1] % CORES
    bf, f32 = jnp.bfloat16, jnp.float32
    scale = 1.0 / math.sqrt(HD)
    c2 = scale * math.log2(math.e)
    span = SEL * HD
    for part in range(4):
        for s in range(SLOTS):
            place = (2 - part // 2 * 2) + (x ^ (s // 2))
            kv[place * QT + part % 2 * 2 + s % 2] = kv_refs[part][s]
    for s in range(SLOTS):
        qg[(x ^ (s // 2)) * 2 + s % 2] = qg_refs[s][...]

    def bias_of(frame, lag):
        return jnp.where((lag <= frame) & (lag < win[frame]), 0.0, NEG)

    biases = {}
    cols = {}
    for a in range(GROUP):
        for d in range(2):
            j = a * 2 + d
            tile = (y ^ d) * CORES + core
            biases[j] = [bias_of(group * GROUP + a, lag) for lag in range(W)]
            for lag in range(W):
                base = (GROUP + a - lag) * QT
                left = QT * (QT - 1) // 2
                for i in range(SEL):
                    t = tp[lag, tile, i]
                    left = left - t
                    col = ((t % CORES) ^ core) * 2 + ((t // CORES) ^ y)
                    cols[j, lag, i] = col
                    at = (lag * SEL + i) * HD
                    ksel[j, at : at + HD] = kv[base + col, 0]
                    vsel[j, at : at + HD] = kv[base + col, 1]
                cols[j, lag, SEL] = ((left % CORES) ^ core) * 2 + ((left // CORES) ^ y)

    def score(j):
        s = dot(qg[j, 0], ksel[j], ((1,), (1,)))
        return jnp.concatenate(
            [s[:, lag * span : (lag + 1) * span] + biases[j][lag] for lag in range(W)], 1
        )

    def soft(s):
        top = jnp.max(s, -1, keepdims=True)
        e = jnp.exp2((s - top) * c2)
        return e, 1.0 / jnp.sum(e, -1, keepdims=True)

    def spread(ref, j, block):
        a, d = j // 2, j % 2
        for lag in range(W):
            place = GROUP + a - lag
            row = d * HD + (a * 2 * HD if 0 < place < 3 else 0)
            for i in range(SEL):
                at = (lag * SEL + i) * HD
                ref[place * QT + cols[j, lag, i], row : row + HD] = block[:, at : at + HD]
            ref[place * QT + cols[j, lag, SEL], row : row + HD] = jnp.zeros((HD, HD), bf)

    def rest_of(j, e, inv, dprob):
        gf = qg[j, 1].astype(f32)
        e_b = e.astype(bf)
        out = dot(e_b, vsel[j], ((1,), (0,))) * inv
        delta = jnp.sum(gf * out, -1, keepdims=True)
        spread(probs, j, e_b)
        ds = (e * (dprob - delta)).astype(bf)
        spread(dscores, j, ds)
        aq[j, 0] = out.astype(bf)
        aq[j, 1] = (dot(ds, ksel[j], ((1,), (0,))) * (inv * scale)).astype(bf)
        scaled[0, j * HD : (j + 1) * HD] = (qg[j, 0].astype(f32) * inv).astype(bf)
        scaled[1, j * HD : (j + 1) * HD] = (gf * inv).astype(bf)

    def grads(place):
        low, rows = {0: (0, 2 * HD), 1: (0, 4 * HD), 2: (0, 4 * HD), 3: (2 * HD, 2 * HD)}[place]
        to = ((place % 2) ^ x) * 2
        for n, ref in enumerate((dscores, probs)):
            right = jnp.concatenate([ref[place * QT + c, :rows] for c in range(QT)], 1)
            got = dot(scaled[n, low : low + rows], right, ((0,), (0,)))
            for c in range(QT):
                block = got[:, c * HD : (c + 1) * HD].T
                block = block * scale if n == 0 else block
                if c < 2:
                    (own_f if place >= GROUP else halo_f)[to + c, n] = block
                else:
                    first = 0 if place >= GROUP else SLOTS
                    sent_b[first + to + c - 2, n] = block.astype(bf)

    s = score(0)
    for j in range(SLOTS):
        dprob = dot(qg[j, 1], vsel[j], ((1,), (1,)))
        e, inv = soft(s)
        if j + 1 < SLOTS:
            s = score(j + 1)
        rest_of(j, e, inv, dprob)
        if j == 1:
            grads(0)
    for place in range(1, 4):
        grads(place)
    for s in range(SLOTS):
        aq_refs[s][...] = aq[(x ^ (s // 2)) * 2 + s % 2]


def attend(me, tp, win, own, other, halo, halo_other, qg, qg_at):
    nh, rows = own.shape[1], own.shape[3]
    smem = pl.BlockSpec(memory_space=pltpu.SMEM)
    kv_spec = pl.BlockSpec((SLOTS, None, 2, rows, HD), lambda h: (0, h, 0, 0, 0))
    both_spec = pl.BlockSpec((2 * SLOTS, None, 2, rows, HD), lambda h: (0, h, 0, 0, 0))
    qg_spec = pl.BlockSpec((None, 2, rows, HD), lambda h: (h + qg_at, 0, 0, 0))
    aq_spec = pl.BlockSpec((None, 2, rows, HD), lambda h: (h, 0, 0, 0))
    bf, f32 = jnp.bfloat16, jnp.float32
    count = W * SEL * rows
    outs = pl.pallas_call(
        attend_kernel,
        grid=(nh,),
        out_shape=[jax.ShapeDtypeStruct((nh, 2, rows, HD), bf)] * 4
        + [
            jax.ShapeDtypeStruct((SLOTS, nh, 2, rows, HD), f32),
            jax.ShapeDtypeStruct((SLOTS, nh, 2, rows, HD), f32),
            jax.ShapeDtypeStruct((2 * SLOTS, nh, 2, rows, HD), bf),
        ],
        in_specs=[smem] * 3 + [kv_spec] * 4 + [qg_spec] * 4,
        out_specs=[aq_spec] * 4 + [kv_spec] * 2 + [both_spec],
        scratch_shapes=[
            pltpu.VMEM((2 * GROUP * QT, 2, rows, HD), bf),
            pltpu.VMEM((SLOTS, 2, rows, HD), bf),
            pltpu.VMEM((SLOTS, 2, rows, HD), bf),
            pltpu.VMEM((2, SLOTS * rows, HD), bf),
            pltpu.VMEM((SLOTS, count, HD), bf),
            pltpu.VMEM((SLOTS, count, HD), bf),
            pltpu.VMEM((2 * GROUP * QT, SLOTS * rows, HD), bf),
            pltpu.VMEM((2 * GROUP * QT, SLOTS * rows, HD), bf),
        ],
        compiler_params=params(),
        cost_estimate=pl.CostEstimate(flops=1, bytes_accessed=1, transcendentals=0),
    )(me, tp, win, own, other, halo, halo_other, *qg)
    return outs[:4], outs[4:]


def exchange(pieces):
    return [pieces[0]] + [to_slot(pieces[s], s) for s in range(1, SLOTS)]


def shards(query, keys, values, grad_out, tile_pattern, window):
    width = query.shape[1]
    per_chip = width // HD // (GROUP * (lax.axis_size("head") // CORES))
    na = min(FIRST, per_chip - 1)
    nb = per_chip - na
    me = where_am_i()
    f32, bf = jnp.float32, jnp.bfloat16
    heads = range(per_chip)

    def summed(own_f, mine, later):
        return [
            (own_f[s] + mine[s].astype(f32) + later[s].astype(f32)).astype(bf)
            for s in range(SLOTS)
        ]

    def backward(halo_f, sent_b):
        mine = to_core(sent_b)
        back = (halo_f + mine[SLOTS:].astype(f32)).astype(bf)
        return mine, back, to_group(back, -1)

    kv_a = exchange(pack(me, [keys, values], [(0, h) for h in heads[:na]], per_chip))
    own_a = jnp.stack(kv_a)
    halo_a = to_group(own_a, 1)
    other_a = to_core(own_a)
    mixed = exchange(
        pack(
            me,
            [query, grad_out, keys, values],
            [(0, h) for h in heads[:na]] + [(2, h) for h in heads[na:]],
            per_chip,
            after=kv_a[1:],
        )
    )
    mixed, halo_a = lax.optimization_barrier((mixed, halo_a))
    own_b = jnp.stack([p[na:] for p in mixed])
    halo_b = to_group(own_b, 1)
    other_b = to_core(own_b)
    qg_b = exchange(
        pack(me, [query, grad_out], [(0, h) for h in heads[na:]], per_chip, after=mixed[1:])
    )
    halo_other_a = to_core(halo_a)
    aq_a, (own_fa, halo_fa, sent_a) = attend(
        me, tile_pattern, window, own_a, other_a, halo_a, halo_other_a, mixed, 0
    )
    sent_a, qg_b, halo_b = lax.optimization_barrier((sent_a, qg_b, halo_b))
    mine_a, back_a, later_a = backward(halo_fa, sent_a)
    got_aq_a = exchange(aq_a)
    halo_other_b = to_core(halo_b)
    qg_b, back_a = lax.optimization_barrier((qg_b, back_a))
    aq_b, (own_fb, halo_fb, sent_b) = attend(
        me, tile_pattern, window, own_b, other_b, halo_b, halo_other_b, qg_b, 0
    )
    sent_b, later_a, got_aq_a = lax.optimization_barrier((sent_b, later_a, got_aq_a))
    mine_b, _, later_b = backward(halo_fb, sent_b)
    total_a = summed(own_fa, mine_a, later_a)
    got_mixed = exchange([jnp.concatenate([aq_b[s], total_a[s]]) for s in range(SLOTS)])
    attended, grad_query = unpack(
        me,
        [got_aq_a, got_mixed],
        [(0, n) for n in range(na)] + [(1, n) for n in range(nb)],
        per_chip,
        width,
    )
    got_b = exchange(summed(own_fb, mine_b, later_b))
    grad_keys, grad_values = unpack(
        me,
        [got_mixed, got_b],
        [(0, nb + n) for n in range(na)] + [(1, n) for n in range(nb)],
        per_chip,
        width,
    )
    return (attended, grad_query, grad_keys, grad_values)


def solution(mesh):
    placed = P(AXES, None)
    return jax.shard_map(
        shards,
        mesh=mesh,
        in_specs=(placed,) * 4 + (P(), P()),
        out_specs=(placed,) * 4,
        check_vma=False,
    )
```

```python
import math

import jax
import jax.numpy as jnp
from jax import lax
from jax.experimental import pallas as pl
from jax.experimental.pallas import tpu as pltpu
from jax.sharding import PartitionSpec as P

HD = 128
QT = 4
SEL = 3
W = 3
GROUP = 2
CORES = 2
SLOTS = 4
FIRST = 2
NEG = -1e30
AXES = ("tm", "head")


def params(limit=32):
    return pltpu.CompilerParams(vmem_limit_bytes=limit * 2**20)


def moved(block, to):
    frames, heads = lax.axis_size("tm"), lax.axis_size("head")
    route = []
    for t in range(frames):
        for h in range(heads):
            t2, h2 = to(t, h)
            route.append((t * heads + h, t2 % frames * heads + h2))
    return lax.ppermute(block, AXES, route)


def to_slot(block, slot):
    return moved(block, lambda t, h: (t ^ (slot // 2), h ^ (slot % 2 * CORES)))


def to_core(block):
    return moved(block, lambda t, h: (t, h ^ 1))


def to_group(block, step):
    return moved(block, lambda t, h: (t + step * GROUP, h))


def place():
    t, h = lax.axis_index("tm"), lax.axis_index("head")
    return t // GROUP, t % GROUP, h // CORES, h % CORES


def where_am_i():
    t, h = lax.axis_index("tm"), lax.axis_index("head")
    return jnp.stack([t, h]).astype(jnp.int32)


def columns(me, ref, per_chip, slot):
    x, y = me[0] % GROUP, me[1] // CORES
    tiles = ref.shape[1] // (HD * per_chip * GROUP)
    chip = (x ^ (slot // 2)) * tiles + (y ^ (slot % 2))
    return lambda head: pl.ds(pl.multiple_of((chip * per_chip + head) * HD, HD), HD)


def pack_kernel(plan, per_chip, used, me, *refs):
    outs = refs[used:]
    for slot in range(SLOTS):
        at = columns(me, refs[0], per_chip, slot)
        for n, (first, head) in enumerate(plan):
            outs[slot][n, 0] = refs[first][:, at(head)]
            outs[slot][n, 1] = refs[first + 1][:, at(head)]


def pack(me, arrays, plan, per_chip, after=()):
    rows = arrays[0].shape[0]
    shape = jax.ShapeDtypeStruct((len(plan), 2, rows, HD), arrays[0].dtype)
    vmem = pl.BlockSpec(memory_space=pltpu.VMEM)
    used = len(arrays) + len(after)
    return pl.pallas_call(
        lambda *refs: pack_kernel(plan, per_chip, used, *refs),
        out_shape=[shape] * SLOTS,
        in_specs=[pl.BlockSpec(memory_space=pltpu.SMEM)]
        + [vmem] * len(arrays)
        + [pl.BlockSpec(memory_space=pl.ANY)] * len(after),
        out_specs=[vmem] * SLOTS,
        compiler_params=params(),
    )(me, *arrays, *after)


def unpack_kernel(places, per_chip, me, *refs):
    a_ref, b_ref = refs[-2:]
    for slot in range(SLOTS):
        at = columns(me, a_ref, per_chip, slot)
        for head, (group, n) in enumerate(places):
            ref = refs[group * SLOTS + slot]
            a_ref[:, at(head)] = ref[n, 0]
            b_ref[:, at(head)] = ref[n, 1]


def unpack(me, groups, places, per_chip, width):
    flat = [p for group in groups for p in group]
    rows = flat[0].shape[2]
    vmem = pl.BlockSpec(memory_space=pltpu.VMEM)
    return pl.pallas_call(
        lambda *refs: unpack_kernel(places, per_chip, *refs),
        out_shape=[jax.ShapeDtypeStruct((rows, width), flat[0].dtype)] * 2,
        in_specs=[pl.BlockSpec(memory_space=pltpu.SMEM)] + [vmem] * len(flat),
        out_specs=[vmem] * 2,
        compiler_params=params(),
    )(me, *flat)


def dot(a, b, dims):
    return lax.dot_general(a, b, (dims, ((), ())), preferred_element_type=jnp.float32)


def attend_kernel(me, tp, win, *refs):
    kv_refs = refs[:4]
    qg_refs = refs[4:8]
    aq_refs = refs[8:12]
    own_f, halo_f, sent_b = refs[12:15]
    kv, qg, aq, scaled, ksel, vsel, probs, dscores = refs[15:]
    group, x = me[0] // GROUP, me[0] % GROUP
    y, core = me[1] // CORES, me[1] % CORES
    bf, f32 = jnp.bfloat16, jnp.float32
    scale = 1.0 / math.sqrt(HD)
    c2 = scale * math.log2(math.e)
    span = SEL * HD
    for part in range(4):
        for s in range(SLOTS):
            place = (2 - part // 2 * 2) + (x ^ (s // 2))
            kv[place * QT + part % 2 * 2 + s % 2] = kv_refs[part][s]
    for s in range(SLOTS):
        qg[(x ^ (s // 2)) * 2 + s % 2] = qg_refs[s][...]

    def bias_of(frame, lag):
        return jnp.where((lag <= frame) & (lag < win[frame]), 0.0, NEG)

    biases = {}
    cols = {}
    for a in range(GROUP):
        for d in range(2):
            j = a * 2 + d
            tile = (y ^ d) * CORES + core
            biases[j] = [bias_of(group * GROUP + a, lag) for lag in range(W)]
            for lag in range(W):
                base = (GROUP + a - lag) * QT
                left = QT * (QT - 1) // 2
                for i in range(SEL):
                    t = tp[lag, tile, i]
                    left = left - t
                    col = ((t % CORES) ^ core) * 2 + ((t // CORES) ^ y)
                    cols[j, lag, i] = col
                    at = (lag * SEL + i) * HD
                    ksel[j, at : at + HD] = kv[base + col, 0]
                    vsel[j, at : at + HD] = kv[base + col, 1]
                cols[j, lag, SEL] = ((left % CORES) ^ core) * 2 + ((left // CORES) ^ y)

    def score(j):
        s = dot(qg[j, 0], ksel[j], ((1,), (1,)))
        return jnp.concatenate(
            [s[:, lag * span : (lag + 1) * span] + biases[j][lag] for lag in range(W)], 1
        )

    def soft(s):
        top = jnp.max(s, -1, keepdims=True)
        e = jnp.exp2((s - top) * c2)
        return e, 1.0 / jnp.sum(e, -1, keepdims=True)

    def spread(ref, j, block):
        a, d = j // 2, j % 2
        for lag in range(W):
            place = GROUP + a - lag
            row = d * HD + (a * 2 * HD if 0 < place < 3 else 0)
            for i in range(SEL):
                at = (lag * SEL + i) * HD
                ref[place * QT + cols[j, lag, i], row : row + HD] = block[:, at : at + HD]
            ref[place * QT + cols[j, lag, SEL], row : row + HD] = jnp.zeros((HD, HD), bf)

    def rest_of(j, e, inv, dprob):
        gf = qg[j, 1].astype(f32)
        e_b = e.astype(bf)
        out = dot(e_b, vsel[j], ((1,), (0,))) * inv
        delta = jnp.sum(gf * out, -1, keepdims=True)
        spread(probs, j, e_b)
        ds = (e * (dprob - delta)).astype(bf)
        spread(dscores, j, ds)
        aq[j, 0] = out.astype(bf)
        aq[j, 1] = (dot(ds, ksel[j], ((1,), (0,))) * (inv * scale)).astype(bf)
        scaled[0, j * HD : (j + 1) * HD] = (qg[j, 0].astype(f32) * inv).astype(bf)
        scaled[1, j * HD : (j + 1) * HD] = (gf * inv).astype(bf)

    def grads(place):
        low, rows = {0: (0, 2 * HD), 1: (0, 4 * HD), 2: (0, 4 * HD), 3: (2 * HD, 2 * HD)}[place]
        to = ((place % 2) ^ x) * 2
        for n, ref in enumerate((dscores, probs)):
            right = jnp.concatenate([ref[place * QT + c, :rows] for c in range(QT)], 1)
            got = dot(scaled[n, low : low + rows], right, ((0,), (0,)))
            for c in range(QT):
                block = got[:, c * HD : (c + 1) * HD].T
                block = block * scale if n == 0 else block
                if c < 2:
                    (own_f if place >= GROUP else halo_f)[to + c, n] = block
                else:
                    first = 0 if place >= GROUP else SLOTS
                    sent_b[first + to + c - 2, n] = block.astype(bf)

    s = score(0)
    for j in range(SLOTS):
        dprob = dot(qg[j, 1], vsel[j], ((1,), (1,)))
        e, inv = soft(s)
        if j + 1 < SLOTS:
            s = score(j + 1)
        rest_of(j, e, inv, dprob)
        if j == 1:
            grads(0)
    for place in range(1, 4):
        grads(place)
    for s in range(SLOTS):
        aq_refs[s][...] = aq[(x ^ (s // 2)) * 2 + s % 2]


def attend(me, tp, win, own, other, halo, halo_other, qg, qg_at, kv_at, nh):
    rows = own.shape[3]
    smem = pl.BlockSpec(memory_space=pltpu.SMEM)
    in_spec = pl.BlockSpec((SLOTS, None, 2, rows, HD), lambda h: (0, h + kv_at, 0, 0, 0))
    kv_spec = pl.BlockSpec((SLOTS, None, 2, rows, HD), lambda h: (0, h, 0, 0, 0))
    both_spec = pl.BlockSpec((2 * SLOTS, None, 2, rows, HD), lambda h: (0, h, 0, 0, 0))
    qg_spec = pl.BlockSpec((None, 2, rows, HD), lambda h: (h + qg_at, 0, 0, 0))
    aq_spec = pl.BlockSpec((None, 2, rows, HD), lambda h: (h, 0, 0, 0))
    bf, f32 = jnp.bfloat16, jnp.float32
    count = W * SEL * rows
    outs = pl.pallas_call(
        attend_kernel,
        grid=(nh,),
        out_shape=[jax.ShapeDtypeStruct((nh, 2, rows, HD), bf)] * 4
        + [
            jax.ShapeDtypeStruct((SLOTS, nh, 2, rows, HD), f32),
            jax.ShapeDtypeStruct((SLOTS, nh, 2, rows, HD), f32),
            jax.ShapeDtypeStruct((2 * SLOTS, nh, 2, rows, HD), bf),
        ],
        in_specs=[smem] * 3 + [in_spec] * 4 + [qg_spec] * 4,
        out_specs=[aq_spec] * 4 + [kv_spec] * 2 + [both_spec],
        scratch_shapes=[
            pltpu.VMEM((2 * GROUP * QT, 2, rows, HD), bf),
            pltpu.VMEM((SLOTS, 2, rows, HD), bf),
            pltpu.VMEM((SLOTS, 2, rows, HD), bf),
            pltpu.VMEM((2, SLOTS * rows, HD), bf),
            pltpu.VMEM((SLOTS, count, HD), bf),
            pltpu.VMEM((SLOTS, count, HD), bf),
            pltpu.VMEM((2 * GROUP * QT, SLOTS * rows, HD), bf),
            pltpu.VMEM((2 * GROUP * QT, SLOTS * rows, HD), bf),
        ],
        compiler_params=params(),
        cost_estimate=pl.CostEstimate(flops=1, bytes_accessed=1, transcendentals=0),
    )(me, tp, win, own, other, halo, halo_other, *qg)
    return outs[:4], outs[4:]


def exchange(pieces):
    return [pieces[0]] + [to_slot(pieces[s], s) for s in range(1, SLOTS)]


def shards(query, keys, values, grad_out, tile_pattern, window):
    width = query.shape[1]
    per_chip = width // HD // (GROUP * (lax.axis_size("head") // CORES))
    na = min(FIRST, per_chip - 2)
    nb = per_chip - na
    nc = max(1, nb - na)
    me = where_am_i()
    f32, bf = jnp.float32, jnp.bfloat16
    heads = range(per_chip)

    def summed(own_f, mine, later):
        return [
            (own_f[s] + mine[s].astype(f32) + later[s].astype(f32)).astype(bf)
            for s in range(SLOTS)
        ]

    def backward(halo_f, sent_b):
        mine = to_core(sent_b)
        back = (halo_f + mine[SLOTS:].astype(f32)).astype(bf)
        return mine, back, to_group(back, -1)

    kv_a = exchange(pack(me, [keys, values], [(0, h) for h in heads[:na]], per_chip))
    own_a = jnp.stack(kv_a)
    halo_a = to_group(own_a, 1)
    other_a = to_core(own_a)
    mixed = exchange(
        pack(
            me,
            [query, grad_out, keys, values],
            [(0, h) for h in heads[:na]] + [(2, h) for h in heads[na:]],
            per_chip,
            after=kv_a[1:],
        )
    )
    mixed, halo_a = lax.optimization_barrier((mixed, halo_a))
    own_b = jnp.stack([p[na:] for p in mixed])
    halo_b = to_group(own_b, 1)
    other_b = to_core(own_b)
    qg_b = exchange(
        pack(me, [query, grad_out], [(0, h) for h in heads[na:]], per_chip, after=mixed[1:])
    )
    halo_other_a = to_core(halo_a)
    aq_a, (own_fa, halo_fa, sent_a) = attend(
        me, tile_pattern, window, own_a, other_a, halo_a, halo_other_a, mixed, 0, 0, na
    )
    sent_a, qg_b, halo_b = lax.optimization_barrier((sent_a, qg_b, halo_b))
    mine_a, back_a, later_a = backward(halo_fa, sent_a)
    got_aq_a = exchange(aq_a)
    halo_other_b = to_core(halo_b)
    qg_b, back_a = lax.optimization_barrier((qg_b, back_a))
    aq_b, (own_fb, halo_fb, sent_b) = attend(
        me, tile_pattern, window, own_b, other_b, halo_b, halo_other_b, qg_b, 0, 0, nb - nc
    )
    sent_b, later_a, got_aq_a = lax.optimization_barrier((sent_b, later_a, got_aq_a))
    mine_b, back_b, later_b = backward(halo_fb, sent_b)
    qg_b, sent_b = lax.optimization_barrier((qg_b, sent_b))
    aq_c, (own_fc, halo_fc, sent_c) = attend(
        me, tile_pattern, window, own_b, other_b, halo_b, halo_other_b, qg_b, nb - nc, nb - nc, nc
    )
    sent_c, mine_b = lax.optimization_barrier((sent_c, mine_b))
    mine_c, _, later_c = backward(halo_fc, sent_c)
    total_a = summed(own_fa, mine_a, later_a)
    got_mixed = exchange(
        [jnp.concatenate([aq_b[s], aq_c[s], total_a[s]]) for s in range(SLOTS)]
    )
    attended, grad_query = unpack(
        me,
        [got_aq_a, got_mixed],
        [(0, n) for n in range(na)] + [(1, n) for n in range(nb)],
        per_chip,
        width,
    )
    got_b = exchange(summed(own_fb, mine_b, later_b))
    got_c = exchange(summed(own_fc, mine_c, later_c))
    grad_keys, grad_values = unpack(
        me,
        [got_mixed, got_b, got_c],
        [(0, nb + n) for n in range(na)]
        + [(1, n) for n in range(nb - nc)]
        + [(2, n) for n in range(nc)],
        per_chip,
        width,
    )
    return (attended, grad_query, grad_keys, grad_values)


def solution(mesh):
    placed = P(AXES, None)
    return jax.shard_map(
        shards,
        mesh=mesh,
        in_specs=(placed,) * 4 + (P(), P()),
        out_specs=(placed,) * 4,
        check_vma=False,
    )
```

```python
import math

import jax
import jax.numpy as jnp
from jax import lax
from jax.experimental import pallas as pl
from jax.experimental.pallas import tpu as pltpu
from jax.sharding import PartitionSpec as P

HD = 128
QT = 4
SEL = 3
W = 3
GROUP = 2
CORES = 2
SLOTS = 4
FIRST = 2
NEG = -1e30
AXES = ("tm", "head")


def params(limit=32):
    return pltpu.CompilerParams(vmem_limit_bytes=limit * 2**20)


def moved(block, to):
    frames, heads = lax.axis_size("tm"), lax.axis_size("head")
    route = []
    for t in range(frames):
        for h in range(heads):
            t2, h2 = to(t, h)
            route.append((t * heads + h, t2 % frames * heads + h2))
    return lax.ppermute(block, AXES, route)


def to_slot(block, slot):
    return moved(block, lambda t, h: (t ^ (slot // 2), h ^ (slot % 2 * CORES)))


def to_core(block):
    return moved(block, lambda t, h: (t, h ^ 1))


def to_group(block, step):
    return moved(block, lambda t, h: (t + step * GROUP, h))


def place():
    t, h = lax.axis_index("tm"), lax.axis_index("head")
    return t // GROUP, t % GROUP, h // CORES, h % CORES


def where_am_i():
    t, h = lax.axis_index("tm"), lax.axis_index("head")
    return jnp.stack([t, h]).astype(jnp.int32)


def columns(me, ref, per_chip, slot):
    x, y = me[0] % GROUP, me[1] // CORES
    tiles = ref.shape[1] // (HD * per_chip * GROUP)
    chip = (x ^ (slot // 2)) * tiles + (y ^ (slot % 2))
    return lambda head: pl.ds(pl.multiple_of((chip * per_chip + head) * HD, HD), HD)


def pack_kernel(plan, per_chip, used, me, *refs):
    outs = refs[used:]
    for slot in range(SLOTS):
        at = columns(me, refs[0], per_chip, slot)
        for n, (first, head) in enumerate(plan):
            outs[slot][n, 0] = refs[first][:, at(head)]
            outs[slot][n, 1] = refs[first + 1][:, at(head)]


def pack(me, arrays, plan, per_chip, after=()):
    rows = arrays[0].shape[0]
    shape = jax.ShapeDtypeStruct((len(plan), 2, rows, HD), arrays[0].dtype)
    vmem = pl.BlockSpec(memory_space=pltpu.VMEM)
    used = len(arrays) + len(after)
    return pl.pallas_call(
        lambda *refs: pack_kernel(plan, per_chip, used, *refs),
        out_shape=[shape] * SLOTS,
        in_specs=[pl.BlockSpec(memory_space=pltpu.SMEM)]
        + [vmem] * len(arrays)
        + [pl.BlockSpec(memory_space=pl.ANY)] * len(after),
        out_specs=[vmem] * SLOTS,
        compiler_params=params(),
    )(me, *arrays, *after)


def unpack_kernel(places, per_chip, me, *refs):
    a_ref, b_ref = refs[-2:]
    for slot in range(SLOTS):
        at = columns(me, a_ref, per_chip, slot)
        for head, (group, n) in enumerate(places):
            ref = refs[group * SLOTS + slot]
            a_ref[:, at(head)] = ref[n, 0]
            b_ref[:, at(head)] = ref[n, 1]


def unpack(me, groups, places, per_chip, width):
    flat = [p for group in groups for p in group]
    rows = flat[0].shape[2]
    vmem = pl.BlockSpec(memory_space=pltpu.VMEM)
    return pl.pallas_call(
        lambda *refs: unpack_kernel(places, per_chip, *refs),
        out_shape=[jax.ShapeDtypeStruct((rows, width), flat[0].dtype)] * 2,
        in_specs=[pl.BlockSpec(memory_space=pltpu.SMEM)] + [vmem] * len(flat),
        out_specs=[vmem] * 2,
        compiler_params=params(),
    )(me, *flat)


def dot(a, b, dims):
    return lax.dot_general(a, b, (dims, ((), ())), preferred_element_type=jnp.float32)


def attend_kernel(me, tp, win, *refs):
    kv_refs = refs[:4]
    qg_refs = refs[4:8]
    aq_refs = refs[8:12]
    own_f, halo_f, sent_b = refs[12:15]
    kv, qg, aq, scaled, ksel, vsel, probs, dscores = refs[15:]
    group, x = me[0] // GROUP, me[0] % GROUP
    y, core = me[1] // CORES, me[1] % CORES
    bf, f32 = jnp.bfloat16, jnp.float32
    scale = 1.0 / math.sqrt(HD)
    c2 = scale * math.log2(math.e)
    span = SEL * HD
    for part in range(4):
        for s in range(SLOTS):
            place = (2 - part // 2 * 2) + (x ^ (s // 2))
            kv[place * QT + part % 2 * 2 + s % 2] = kv_refs[part][s]
    for s in range(SLOTS):
        qg[(x ^ (s // 2)) * 2 + s % 2] = qg_refs[s][...]

    def bias_of(frame, lag):
        return jnp.where((lag <= frame) & (lag < win[frame]), 0.0, NEG)

    biases = {}
    cols = {}
    for a in range(GROUP):
        for d in range(2):
            j = a * 2 + d
            tile = (y ^ d) * CORES + core
            biases[j] = [bias_of(group * GROUP + a, lag) for lag in range(W)]
            for lag in range(W):
                base = (GROUP + a - lag) * QT
                left = QT * (QT - 1) // 2
                for i in range(SEL):
                    t = tp[lag, tile, i]
                    left = left - t
                    col = ((t % CORES) ^ core) * 2 + ((t // CORES) ^ y)
                    cols[j, lag, i] = col
                    at = (lag * SEL + i) * HD
                    ksel[j, at : at + HD] = kv[base + col, 0]
                    vsel[j, at : at + HD] = kv[base + col, 1]
                cols[j, lag, SEL] = ((left % CORES) ^ core) * 2 + ((left // CORES) ^ y)

    def score(j):
        s = dot(qg[j, 0], ksel[j], ((1,), (1,)))
        return jnp.concatenate(
            [s[:, lag * span : (lag + 1) * span] + biases[j][lag] for lag in range(W)], 1
        )

    def soft(s):
        top = jnp.max(s, -1, keepdims=True)
        e = jnp.exp2((s - top) * c2)
        return e, 1.0 / jnp.sum(e, -1, keepdims=True)

    def spread(ref, j, block):
        a, d = j // 2, j % 2
        for lag in range(W):
            place = GROUP + a - lag
            row = d * HD + (a * 2 * HD if 0 < place < 3 else 0)
            for i in range(SEL):
                at = (lag * SEL + i) * HD
                ref[place * QT + cols[j, lag, i], row : row + HD] = block[:, at : at + HD]
            ref[place * QT + cols[j, lag, SEL], row : row + HD] = jnp.zeros((HD, HD), bf)

    def rest_of(j, e, inv, dprob):
        gf = qg[j, 1].astype(f32)
        e_b = e.astype(bf)
        out = dot(e_b, vsel[j], ((1,), (0,))) * inv
        delta = jnp.sum(gf * out, -1, keepdims=True)
        spread(probs, j, e_b)
        ds = (e * (dprob - delta)).astype(bf)
        spread(dscores, j, ds)
        aq[j, 0] = out.astype(bf)
        aq[j, 1] = (dot(ds, ksel[j], ((1,), (0,))) * (inv * scale)).astype(bf)
        scaled[0, j * HD : (j + 1) * HD] = (qg[j, 0].astype(f32) * inv).astype(bf)
        scaled[1, j * HD : (j + 1) * HD] = (gf * inv).astype(bf)

    def grads(place):
        low, rows = {0: (0, 2 * HD), 1: (0, 4 * HD), 2: (0, 4 * HD), 3: (2 * HD, 2 * HD)}[place]
        to = ((place % 2) ^ x) * 2
        for n, ref in enumerate((dscores, probs)):
            right = jnp.concatenate([ref[place * QT + c, :rows] for c in range(QT)], 1)
            got = dot(scaled[n, low : low + rows], right, ((0,), (0,)))
            for c in range(QT):
                block = got[:, c * HD : (c + 1) * HD].T
                block = block * scale if n == 0 else block
                if c < 2:
                    (own_f if place >= GROUP else halo_f)[to + c, n] = block
                else:
                    first = 0 if place >= GROUP else SLOTS
                    sent_b[first + to + c - 2, n] = block.astype(bf)

    s = score(0)
    dprob = dot(qg[0, 1], vsel[0], ((1,), (1,)))
    for j in range(SLOTS):
        e, inv = soft(s)
        this = dprob
        if j + 1 < SLOTS:
            s = score(j + 1)
            dprob = dot(qg[j + 1, 1], vsel[j + 1], ((1,), (1,)))
        rest_of(j, e, inv, this)
        if j == 1:
            grads(0)
    for place in range(1, 4):
        grads(place)
    for s in range(SLOTS):
        aq_refs[s][...] = aq[(x ^ (s // 2)) * 2 + s % 2]


def attend(me, tp, win, own, other, halo, halo_other, qg, qg_at, kv_at, nh):
    rows = own.shape[3]
    smem = pl.BlockSpec(memory_space=pltpu.SMEM)
    in_spec = pl.BlockSpec((SLOTS, None, 2, rows, HD), lambda h: (0, h + kv_at, 0, 0, 0))
    kv_spec = pl.BlockSpec((SLOTS, None, 2, rows, HD), lambda h: (0, h, 0, 0, 0))
    both_spec = pl.BlockSpec((2 * SLOTS, None, 2, rows, HD), lambda h: (0, h, 0, 0, 0))
    qg_spec = pl.BlockSpec((None, 2, rows, HD), lambda h: (h + qg_at, 0, 0, 0))
    aq_spec = pl.BlockSpec((None, 2, rows, HD), lambda h: (h, 0, 0, 0))
    bf, f32 = jnp.bfloat16, jnp.float32
    count = W * SEL * rows
    outs = pl.pallas_call(
        attend_kernel,
        grid=(nh,),
        out_shape=[jax.ShapeDtypeStruct((nh, 2, rows, HD), bf)] * 4
        + [
            jax.ShapeDtypeStruct((SLOTS, nh, 2, rows, HD), f32),
            jax.ShapeDtypeStruct((SLOTS, nh, 2, rows, HD), f32),
            jax.ShapeDtypeStruct((2 * SLOTS, nh, 2, rows, HD), bf),
        ],
        in_specs=[smem] * 3 + [in_spec] * 4 + [qg_spec] * 4,
        out_specs=[aq_spec] * 4 + [kv_spec] * 2 + [both_spec],
        scratch_shapes=[
            pltpu.VMEM((2 * GROUP * QT, 2, rows, HD), bf),
            pltpu.VMEM((SLOTS, 2, rows, HD), bf),
            pltpu.VMEM((SLOTS, 2, rows, HD), bf),
            pltpu.VMEM((2, SLOTS * rows, HD), bf),
            pltpu.VMEM((SLOTS, count, HD), bf),
            pltpu.VMEM((SLOTS, count, HD), bf),
            pltpu.VMEM((2 * GROUP * QT, SLOTS * rows, HD), bf),
            pltpu.VMEM((2 * GROUP * QT, SLOTS * rows, HD), bf),
        ],
        compiler_params=params(),
        cost_estimate=pl.CostEstimate(flops=1, bytes_accessed=1, transcendentals=0),
    )(me, tp, win, own, other, halo, halo_other, *qg)
    return outs[:4], outs[4:]


def exchange(pieces):
    return [pieces[0]] + [to_slot(pieces[s], s) for s in range(1, SLOTS)]


def shards(query, keys, values, grad_out, tile_pattern, window):
    width = query.shape[1]
    per_chip = width // HD // (GROUP * (lax.axis_size("head") // CORES))
    na = min(FIRST, per_chip - 2)
    nb = per_chip - na
    nc = max(1, nb - na)
    me = where_am_i()
    f32, bf = jnp.float32, jnp.bfloat16
    heads = range(per_chip)

    def summed(own_f, mine, later):
        return [
            (own_f[s] + mine[s].astype(f32) + later[s].astype(f32)).astype(bf)
            for s in range(SLOTS)
        ]

    def backward(halo_f, sent_b):
        mine = to_core(sent_b)
        back = (halo_f + mine[SLOTS:].astype(f32)).astype(bf)
        return mine, back, to_group(back, -1)

    kv_a = exchange(pack(me, [keys, values], [(0, h) for h in heads[:na]], per_chip))
    own_a = jnp.stack(kv_a)
    halo_a = to_group(own_a, 1)
    other_a = to_core(own_a)
    mixed = exchange(
        pack(
            me,
            [query, grad_out, keys, values],
            [(0, h) for h in heads[:na]] + [(2, h) for h in heads[na:]],
            per_chip,
            after=kv_a[1:],
        )
    )
    mixed, halo_a = lax.optimization_barrier((mixed, halo_a))
    own_b = jnp.stack([p[na:] for p in mixed])
    halo_b = to_group(own_b, 1)
    other_b = to_core(own_b)
    qg_b = exchange(
        pack(me, [query, grad_out], [(0, h) for h in heads[na:]], per_chip, after=mixed[1:])
    )
    halo_other_a = to_core(halo_a)
    aq_a, (own_fa, halo_fa, sent_a) = attend(
        me, tile_pattern, window, own_a, other_a, halo_a, halo_other_a, mixed, 0, 0, na
    )
    sent_a, qg_b, halo_b = lax.optimization_barrier((sent_a, qg_b, halo_b))
    mine_a, back_a, later_a = backward(halo_fa, sent_a)
    got_aq_a = exchange(aq_a)
    halo_other_b = to_core(halo_b)
    qg_b, back_a = lax.optimization_barrier((qg_b, back_a))
    aq_b, (own_fb, halo_fb, sent_b) = attend(
        me, tile_pattern, window, own_b, other_b, halo_b, halo_other_b, qg_b, 0, 0, nb - nc
    )
    sent_b, later_a, got_aq_a = lax.optimization_barrier((sent_b, later_a, got_aq_a))
    mine_b, back_b, later_b = backward(halo_fb, sent_b)
    qg_b, sent_b = lax.optimization_barrier((qg_b, sent_b))
    aq_c, (own_fc, halo_fc, sent_c) = attend(
        me, tile_pattern, window, own_b, other_b, halo_b, halo_other_b, qg_b, nb - nc, nb - nc, nc
    )
    sent_c, mine_b = lax.optimization_barrier((sent_c, mine_b))
    mine_c, _, later_c = backward(halo_fc, sent_c)
    total_a = summed(own_fa, mine_a, later_a)
    got_mixed = exchange(
        [jnp.concatenate([aq_b[s], aq_c[s], total_a[s]]) for s in range(SLOTS)]
    )
    attended, grad_query = unpack(
        me,
        [got_aq_a, got_mixed],
        [(0, n) for n in range(na)] + [(1, n) for n in range(nb)],
        per_chip,
        width,
    )
    got_b = exchange(summed(own_fb, mine_b, later_b))
    got_c = exchange(summed(own_fc, mine_c, later_c))
    grad_keys, grad_values = unpack(
        me,
        [got_mixed, got_b, got_c],
        [(0, nb + n) for n in range(na)]
        + [(1, n) for n in range(nb - nc)]
        + [(2, n) for n in range(nc)],
        per_chip,
        width,
    )
    return (attended, grad_query, grad_keys, grad_values)


def solution(mesh):
    placed = P(AXES, None)
    return jax.shard_map(
        shards,
        mesh=mesh,
        in_specs=(placed,) * 4 + (P(), P()),
        out_specs=(placed,) * 4,
        check_vma=False,
    )
```

```python
import math

import jax
import jax.numpy as jnp
from jax import lax
from jax.experimental import pallas as pl
from jax.experimental.pallas import tpu as pltpu
from jax.sharding import PartitionSpec as P

HD = 128
QT = 4
SEL = 3
W = 3
GROUP = 2
CORES = 2
SLOTS = 4
FIRST = 2
NEG = -1e30
AXES = ("tm", "head")


def params(limit=32):
    return pltpu.CompilerParams(vmem_limit_bytes=limit * 2**20)


def moved(block, to):
    frames, heads = lax.axis_size("tm"), lax.axis_size("head")
    route = []
    for t in range(frames):
        for h in range(heads):
            t2, h2 = to(t, h)
            route.append((t * heads + h, t2 % frames * heads + h2))
    return lax.ppermute(block, AXES, route)


def to_slot(block, slot):
    return moved(block, lambda t, h: (t ^ (slot // 2), h ^ (slot % 2 * CORES)))


def to_core(block):
    return moved(block, lambda t, h: (t, h ^ 1))


def to_group(block, step):
    return moved(block, lambda t, h: (t + step * GROUP, h))


def place():
    t, h = lax.axis_index("tm"), lax.axis_index("head")
    return t // GROUP, t % GROUP, h // CORES, h % CORES


def where_am_i():
    t, h = lax.axis_index("tm"), lax.axis_index("head")
    return jnp.stack([t, h]).astype(jnp.int32)


def columns(me, ref, per_chip, slot):
    x, y = me[0] % GROUP, me[1] // CORES
    tiles = ref.shape[1] // (HD * per_chip * GROUP)
    chip = (x ^ (slot // 2)) * tiles + (y ^ (slot % 2))
    return lambda head: pl.ds(pl.multiple_of((chip * per_chip + head) * HD, HD), HD)


def pack_kernel(plan, per_chip, used, me, *refs):
    outs = refs[used:]
    for slot in range(SLOTS):
        at = columns(me, refs[0], per_chip, slot)
        for n, (first, head) in enumerate(plan):
            outs[slot][n, 0] = refs[first][:, at(head)]
            outs[slot][n, 1] = refs[first + 1][:, at(head)]


def pack(me, arrays, plan, per_chip, after=()):
    rows = arrays[0].shape[0]
    shape = jax.ShapeDtypeStruct((len(plan), 2, rows, HD), arrays[0].dtype)
    vmem = pl.BlockSpec(memory_space=pltpu.VMEM)
    used = len(arrays) + len(after)
    return pl.pallas_call(
        lambda *refs: pack_kernel(plan, per_chip, used, *refs),
        out_shape=[shape] * SLOTS,
        in_specs=[pl.BlockSpec(memory_space=pltpu.SMEM)]
        + [vmem] * len(arrays)
        + [pl.BlockSpec(memory_space=pl.ANY)] * len(after),
        out_specs=[vmem] * SLOTS,
        compiler_params=params(),
    )(me, *arrays, *after)


def unpack_kernel(places, per_chip, me, *refs):
    a_ref, b_ref = refs[-2:]
    for slot in range(SLOTS):
        at = columns(me, a_ref, per_chip, slot)
        for head, (group, n) in enumerate(places):
            ref = refs[group * SLOTS + slot]
            a_ref[:, at(head)] = ref[n, 0]
            b_ref[:, at(head)] = ref[n, 1]


def unpack(me, groups, places, per_chip, width):
    flat = [p for group in groups for p in group]
    rows = flat[0].shape[2]
    vmem = pl.BlockSpec(memory_space=pltpu.VMEM)
    return pl.pallas_call(
        lambda *refs: unpack_kernel(places, per_chip, *refs),
        out_shape=[jax.ShapeDtypeStruct((rows, width), flat[0].dtype)] * 2,
        in_specs=[pl.BlockSpec(memory_space=pltpu.SMEM)] + [vmem] * len(flat),
        out_specs=[vmem] * 2,
        compiler_params=params(),
    )(me, *flat)


def dot(a, b, dims):
    return lax.dot_general(a, b, (dims, ((), ())), preferred_element_type=jnp.float32)


def attend_kernel(me, tp, win, *refs):
    kv_refs = refs[:4]
    qg_refs = refs[4:8]
    aq_refs = refs[8:12]
    own_f, halo_f, sent_b = refs[12:15]
    kv, qg, aq, scaled, ksel, vsel, probs, dscores = refs[15:]
    group, x = me[0] // GROUP, me[0] % GROUP
    y, core = me[1] // CORES, me[1] % CORES
    bf, f32 = jnp.bfloat16, jnp.float32
    scale = 1.0 / math.sqrt(HD)
    c2 = scale * math.log2(math.e)
    span = SEL * HD
    for part in range(4):
        for s in range(SLOTS):
            place = (2 - part // 2 * 2) + (x ^ (s // 2))
            kv[place * QT + part % 2 * 2 + s % 2] = kv_refs[part][s]
    for s in range(SLOTS):
        qg[(x ^ (s // 2)) * 2 + s % 2] = qg_refs[s][...]

    def bias_of(frame, lag):
        return jnp.where((lag <= frame) & (lag < win[frame]), 0.0, NEG)

    biases = {}
    cols = {}
    for a in range(GROUP):
        for d in range(2):
            j = a * 2 + d
            tile = (y ^ d) * CORES + core
            biases[j] = [bias_of(group * GROUP + a, lag) for lag in range(W)]
            for lag in range(W):
                base = (GROUP + a - lag) * QT
                left = QT * (QT - 1) // 2
                for i in range(SEL):
                    t = tp[lag, tile, i]
                    left = left - t
                    col = ((t % CORES) ^ core) * 2 + ((t // CORES) ^ y)
                    cols[j, lag, i] = col
                    at = (lag * SEL + i) * HD
                    ksel[j, at : at + HD] = kv[base + col, 0]
                    vsel[j, at : at + HD] = kv[base + col, 1]
                cols[j, lag, SEL] = ((left % CORES) ^ core) * 2 + ((left // CORES) ^ y)

    def score(j):
        s = dot(qg[j, 0], ksel[j], ((1,), (1,)))
        return jnp.concatenate(
            [s[:, lag * span : (lag + 1) * span] + biases[j][lag] for lag in range(W)], 1
        )

    def soft(s):
        top = jnp.max(s, -1, keepdims=True)
        e = jnp.exp2(s * c2 - top * c2)
        return e, 1.0 / jnp.sum(e, -1, keepdims=True)

    def spread(ref, j, block):
        a, d = j // 2, j % 2
        for lag in range(W):
            place = GROUP + a - lag
            row = d * HD + (a * 2 * HD if 0 < place < 3 else 0)
            for i in range(SEL):
                at = (lag * SEL + i) * HD
                ref[place * QT + cols[j, lag, i], row : row + HD] = block[:, at : at + HD]
            ref[place * QT + cols[j, lag, SEL], row : row + HD] = jnp.zeros((HD, HD), bf)

    def rest_of(j, e, inv, dprob):
        gf = qg[j, 1].astype(f32)
        e_b = e.astype(bf)
        out = dot(e_b, vsel[j], ((1,), (0,))) * inv
        delta = jnp.sum(gf * out, -1, keepdims=True)
        spread(probs, j, e_b)
        ds = (e * (dprob - delta)).astype(bf)
        spread(dscores, j, ds)
        aq[j, 0] = out.astype(bf)
        aq[j, 1] = (dot(ds, ksel[j], ((1,), (0,))) * (inv * scale)).astype(bf)
        scaled[0, j * HD : (j + 1) * HD] = (qg[j, 0].astype(f32) * inv).astype(bf)
        scaled[1, j * HD : (j + 1) * HD] = (gf * inv).astype(bf)

    def grads(place):
        low, rows = {0: (0, 2 * HD), 1: (0, 4 * HD), 2: (0, 4 * HD), 3: (2 * HD, 2 * HD)}[place]
        to = ((place % 2) ^ x) * 2
        for n, ref in enumerate((dscores, probs)):
            right = jnp.concatenate([ref[place * QT + c, :rows] for c in range(QT)], 1)
            got = dot(scaled[n, low : low + rows], right, ((0,), (0,)))
            for c in range(QT):
                block = got[:, c * HD : (c + 1) * HD].T
                block = block * scale if n == 0 else block
                if c < 2:
                    (own_f if place >= GROUP else halo_f)[to + c, n] = block
                else:
                    first = 0 if place >= GROUP else SLOTS
                    sent_b[first + to + c - 2, n] = block.astype(bf)

    s = score(0)
    dprob = dot(qg[0, 1], vsel[0], ((1,), (1,)))
    for j in range(SLOTS):
        e, inv = soft(s)
        this = dprob
        if j + 1 < SLOTS:
            s = score(j + 1)
            dprob = dot(qg[j + 1, 1], vsel[j + 1], ((1,), (1,)))
        rest_of(j, e, inv, this)
        if j == 1:
            grads(0)
    for place in range(1, 4):
        grads(place)
    for s in range(SLOTS):
        aq_refs[s][...] = aq[(x ^ (s // 2)) * 2 + s % 2]


def attend(me, tp, win, own, other, halo, halo_other, qg, qg_at, kv_at, nh):
    rows = own.shape[3]
    smem = pl.BlockSpec(memory_space=pltpu.SMEM)
    in_spec = pl.BlockSpec((SLOTS, None, 2, rows, HD), lambda h: (0, h + kv_at, 0, 0, 0))
    kv_spec = pl.BlockSpec((SLOTS, None, 2, rows, HD), lambda h: (0, h, 0, 0, 0))
    both_spec = pl.BlockSpec((2 * SLOTS, None, 2, rows, HD), lambda h: (0, h, 0, 0, 0))
    qg_spec = pl.BlockSpec((None, 2, rows, HD), lambda h: (h + qg_at, 0, 0, 0))
    aq_spec = pl.BlockSpec((None, 2, rows, HD), lambda h: (h, 0, 0, 0))
    bf, f32 = jnp.bfloat16, jnp.float32
    count = W * SEL * rows
    outs = pl.pallas_call(
        attend_kernel,
        grid=(nh,),
        out_shape=[jax.ShapeDtypeStruct((nh, 2, rows, HD), bf)] * 4
        + [
            jax.ShapeDtypeStruct((SLOTS, nh, 2, rows, HD), f32),
            jax.ShapeDtypeStruct((SLOTS, nh, 2, rows, HD), f32),
            jax.ShapeDtypeStruct((2 * SLOTS, nh, 2, rows, HD), bf),
        ],
        in_specs=[smem] * 3 + [in_spec] * 4 + [qg_spec] * 4,
        out_specs=[aq_spec] * 4 + [kv_spec] * 2 + [both_spec],
        scratch_shapes=[
            pltpu.VMEM((2 * GROUP * QT, 2, rows, HD), bf),
            pltpu.VMEM((SLOTS, 2, rows, HD), bf),
            pltpu.VMEM((SLOTS, 2, rows, HD), bf),
            pltpu.VMEM((2, SLOTS * rows, HD), bf),
            pltpu.VMEM((SLOTS, count, HD), bf),
            pltpu.VMEM((SLOTS, count, HD), bf),
            pltpu.VMEM((2 * GROUP * QT, SLOTS * rows, HD), bf),
            pltpu.VMEM((2 * GROUP * QT, SLOTS * rows, HD), bf),
        ],
        compiler_params=params(),
        cost_estimate=pl.CostEstimate(flops=1, bytes_accessed=1, transcendentals=0),
    )(me, tp, win, own, other, halo, halo_other, *qg)
    return outs[:4], outs[4:]


def exchange(pieces):
    return [pieces[0]] + [to_slot(pieces[s], s) for s in range(1, SLOTS)]


def shards(query, keys, values, grad_out, tile_pattern, window):
    width = query.shape[1]
    per_chip = width // HD // (GROUP * (lax.axis_size("head") // CORES))
    na = min(FIRST, per_chip - 2)
    nb = per_chip - na
    nc = max(1, nb - na)
    me = where_am_i()
    f32, bf = jnp.float32, jnp.bfloat16
    heads = range(per_chip)

    def summed(own_f, mine, later):
        return [
            (own_f[s] + mine[s].astype(f32) + later[s].astype(f32)).astype(bf)
            for s in range(SLOTS)
        ]

    def backward(halo_f, sent_b):
        mine = to_core(sent_b)
        back = (halo_f + mine[SLOTS:].astype(f32)).astype(bf)
        return mine, back, to_group(back, -1)

    kv_a = exchange(pack(me, [keys, values], [(0, h) for h in heads[:na]], per_chip))
    own_a = jnp.stack(kv_a)
    halo_a = to_group(own_a, 1)
    other_a = to_core(own_a)
    mixed = exchange(
        pack(
            me,
            [query, grad_out, keys, values],
            [(0, h) for h in heads[:na]] + [(2, h) for h in heads[na:]],
            per_chip,
            after=kv_a[1:],
        )
    )
    mixed, halo_a = lax.optimization_barrier((mixed, halo_a))
    own_b = jnp.stack([p[na:] for p in mixed])
    halo_b = to_group(own_b, 1)
    other_b = to_core(own_b)
    qg_b = exchange(
        pack(me, [query, grad_out], [(0, h) for h in heads[na:]], per_chip, after=mixed[1:])
    )
    halo_other_a = to_core(halo_a)
    aq_a, (own_fa, halo_fa, sent_a) = attend(
        me, tile_pattern, window, own_a, other_a, halo_a, halo_other_a, mixed, 0, 0, na
    )
    sent_a, qg_b, halo_b = lax.optimization_barrier((sent_a, qg_b, halo_b))
    mine_a, back_a, later_a = backward(halo_fa, sent_a)
    got_aq_a = exchange(aq_a)
    halo_other_b = to_core(halo_b)
    qg_b, back_a = lax.optimization_barrier((qg_b, back_a))
    aq_b, (own_fb, halo_fb, sent_b) = attend(
        me, tile_pattern, window, own_b, other_b, halo_b, halo_other_b, qg_b, 0, 0, nb - nc
    )
    sent_b, later_a, got_aq_a = lax.optimization_barrier((sent_b, later_a, got_aq_a))
    mine_b, back_b, later_b = backward(halo_fb, sent_b)
    qg_b, sent_b = lax.optimization_barrier((qg_b, sent_b))
    aq_c, (own_fc, halo_fc, sent_c) = attend(
        me, tile_pattern, window, own_b, other_b, halo_b, halo_other_b, qg_b, nb - nc, nb - nc, nc
    )
    sent_c, mine_b = lax.optimization_barrier((sent_c, mine_b))
    mine_c, _, later_c = backward(halo_fc, sent_c)
    total_a = summed(own_fa, mine_a, later_a)
    got_mixed = exchange(
        [jnp.concatenate([aq_b[s], aq_c[s], total_a[s]]) for s in range(SLOTS)]
    )
    attended, grad_query = unpack(
        me,
        [got_aq_a, got_mixed],
        [(0, n) for n in range(na)] + [(1, n) for n in range(nb)],
        per_chip,
        width,
    )
    got_b = exchange(summed(own_fb, mine_b, later_b))
    got_c = exchange(summed(own_fc, mine_c, later_c))
    grad_keys, grad_values = unpack(
        me,
        [got_mixed, got_b, got_c],
        [(0, nb + n) for n in range(na)]
        + [(1, n) for n in range(nb - nc)]
        + [(2, n) for n in range(nc)],
        per_chip,
        width,
    )
    return (attended, grad_query, grad_keys, grad_values)


def solution(mesh):
    placed = P(AXES, None)
    return jax.shard_map(
        shards,
        mesh=mesh,
        in_specs=(placed,) * 4 + (P(), P()),
        out_specs=(placed,) * 4,
        check_vma=False,
    )
```
